512 devices in a mesh: seq: 16 (over y_hi, x), dp: 32 (over z, y_lo, core).
Axes of the slice: x: 4, y: 8 (y_hi: 4, y_lo: 2; y = y_hi * 2 + y_lo), z: 8, core: 2. Of those that a mesh axis runs over, the one named last changes fastest.
Arguments:
- queries: bfloat16 [32, 2048, 2048], P('dp', 'seq'), may hold values from -96 to 96
- pool: bfloat16 [32, 96, 128, 896], P('dp', 'seq'), may hold values from -8 to 8
- slots: int32 [32, 32, 2], P('dp', 'seq'), may hold values from 0 to 5
- key_weight: bfloat16 [896, 2048], P('dp'), may hold values from -0.141 to 0.141
- value_weight: bfloat16 [896, 2048], P('dp'), may hold values from -0.1875 to 0.1875
- cotangent: bfloat16 [32, 2048, 2048], P('dp', 'seq'), may hold values from -6 to 6
Outputs:
- attended: bfloat16 [32, 2048, 2048], P('dp', 'seq')
- query_grad: bfloat16 [32, 2048, 2048], P('dp', 'seq')
- value_weight_grad: float32 [896, 2048], P('dp')
The draws below stay inside these ranges and needn't reach their ends.
All inputs are finite; a program needn't handle non-finite values.
Results may differ from the reference program's by a relative error of at most 0.039.
Values may be sent and summed in bfloat16 or wider, within the bound.
No kernel may reach another device: no remote copies, remote signals or barrier semaphores. Data moves between devices by JAX's collectives and lax.ppermute only.
A program may use at most 64 MiB of HBM per device.

```python
import math
import jax
import jax.numpy as jnp
from jax import lax

HEADS = 16
HEAD_DIM = 128
ENC_WIDTH = 896
NEIGHBOURS = 2
NB_LEN = 128
BLOCK = 64
HD = 2048
BLOCKS_DEV = 2
POOL_DEV = 6
SEQ_LEN = 2048
BLOCKS = 32
POOL = 96
BATCH = 32
N_SEQ = 16


def shared_parts(key):
    weight_draw = jnp.clip(jax.random.normal(jax.random.fold_in(key, 102), (ENC_WIDTH, HD), jnp.float32), -4.0, 4.0) / math.sqrt(ENC_WIDTH)
    weight_draw = jnp.clip(weight_draw, -0.14, 0.14)
    return weight_draw


def draw_key_weight(key, part):
    weight_draw = shared_parts(key)
    return weight_draw.astype(jnp.bfloat16)


def draw_pool(key, part):
    key = jax.random.fold_in(key, 5)
    noise_key = jax.random.fold_in(key, 0)
    noise = jax.random.normal(noise_key, (BATCH, POOL, NB_LEN, ENC_WIDTH), jnp.float32)
    values = jnp.clip(noise, -6.0, 6.0)
    return values.astype(jnp.bfloat16)


def draw_queries(key, part):
    key = jax.random.fold_in(key, 7)
    base_key = jax.random.fold_in(key, 0)
    values = 2.0 * jnp.clip(jax.random.normal(base_key, (BATCH, SEQ_LEN, HD), jnp.float32), -4.0, 4.0)
    return values.astype(jnp.bfloat16)


def set_ends(result, key, least, top_value):
    extent = result.shape
    spot = [jax.random.randint(jax.random.fold_in(key, axis), (), 0, extent[axis]) for axis in range(len(extent))]
    result = result.at[tuple(spot)].set(least)
    longest = extent.index(max(extent))
    spot[longest] = (spot[longest] + 1) % extent[longest]
    return result.at[tuple(spot)].set(top_value)


def shard_levels(rng, extent, pieces, smallest, high):
    gain, own = 1.0, jax.random.fold_in(rng, 6)
    for dim, shards_of in pieces:
        draws = jnp.exp(jax.random.uniform(jax.random.fold_in(own, dim), (shards_of,), jnp.float32, smallest / len(pieces), high / len(pieces)))
        gain = gain * jnp.repeat(draws, extent[dim] // shards_of).reshape([-1 if axis == dim else 1 for axis in range(len(extent))])
    return gain


def bell_draw(own_key, dims, deviation, most, shards=(), held_as=jnp.bfloat16):
    entries = deviation * jax.random.normal(own_key, dims, jnp.float32)
    if shards:
        entries = entries * shard_levels(own_key, dims, shards, -0.22, 0.18)
    return jnp.clip(entries, -most, most).astype(held_as)


def setup_inputs(seed: int = 0) -> dict:
    key_of = jax.random.split(jax.random.key(seed), 7)
    return {
        "queries": draw_queries(jax.random.fold_in(key_of[6], 71), 0),
        "pool": draw_pool(jax.random.fold_in(key_of[6], 71), 0),
        "slots": set_ends(jax.random.randint(key_of[2], (BATCH, BLOCKS, NEIGHBOURS), 0, POOL_DEV), jax.random.fold_in(key_of[2], 1), 0, POOL_DEV - 1).astype(jnp.int32),
        "key_weight": draw_key_weight(jax.random.fold_in(key_of[6], 71), 0),
        "value_weight": bell_draw(key_of[4], (ENC_WIDTH, HD), ENC_WIDTH ** -0.5, 0.1875, ((0, 32),)),
        "cotangent": bell_draw(key_of[5], (BATCH, SEQ_LEN, HD), 1.0, 6.0, ((0, 32), (1, 16))),
    }


def neighbour_rows(pool_seq, slots_seq):
    group_base = jnp.arange(BLOCKS, dtype=jnp.int32) // BLOCKS_DEV * POOL_DEV
    slot_index = (slots_seq + group_base[:, None]).astype(jnp.int32)
    encodings = pool_seq[slot_index].reshape(BLOCKS, NEIGHBOURS * NB_LEN, ENC_WIDTH)
    zero_rows = jnp.zeros((1, NEIGHBOURS * NB_LEN, ENC_WIDTH), jnp.bfloat16)
    return jnp.concatenate([zero_rows, encodings[:-1]], axis=0)

def reference(queries, pool, slots, key_weight, value_weight, cotangent):
    span = NEIGHBOURS * NB_LEN
    score_scale = 1.0 / math.sqrt(HEAD_DIM)

    def one_sequence(grad_sum, inputs):
        query_seq, pool_seq, slots_seq, cot_seq = inputs
        earlier = neighbour_rows(pool_seq, slots_seq)
        flat_rows = earlier.reshape(BLOCKS * span, ENC_WIDTH)
        key_rows = jnp.dot(flat_rows, key_weight, preferred_element_type=jnp.float32).astype(jnp.bfloat16)
        value_rows = jnp.dot(flat_rows, value_weight, preferred_element_type=jnp.float32).astype(jnp.bfloat16)
        key_heads = key_rows.reshape(BLOCKS, span, HEADS, HEAD_DIM).astype(jnp.float32)
        value_heads = value_rows.reshape(BLOCKS, span, HEADS, HEAD_DIM).astype(jnp.float32)
        query_heads = query_seq.reshape(BLOCKS, BLOCK, HEADS, HEAD_DIM).astype(jnp.float32)
        out_grad = cot_seq.reshape(BLOCKS, BLOCK, HEADS, HEAD_DIM).astype(jnp.float32)
        scores = jnp.einsum('cqhd,ckhd->chqk', query_heads, key_heads) * score_scale
        attn_probs = jax.nn.softmax(scores, axis=-1)
        probs_low = attn_probs.astype(jnp.bfloat16)
        attended = jnp.einsum('chqk,ckhd->cqhd', probs_low.astype(jnp.float32), value_heads).astype(jnp.bfloat16)
        prob_grad = jnp.einsum('cqhd,ckhd->chqk', out_grad, value_heads)
        row_total = jnp.einsum('cqhd,cqhd->chq', out_grad, attended.astype(jnp.float32))
        score_grad = (score_scale * attn_probs * (prob_grad - row_total[..., None])).astype(jnp.bfloat16)
        query_grad = jnp.einsum('chqk,ckhd->cqhd', score_grad.astype(jnp.float32), key_heads).astype(jnp.bfloat16)
        value_grad = jnp.einsum('chqk,cqhd->ckhd', probs_low.astype(jnp.float32), out_grad).astype(jnp.bfloat16)
        group_rows = earlier.reshape(N_SEQ, BLOCKS_DEV * span, ENC_WIDTH).astype(jnp.float32)
        group_grads = value_grad.reshape(N_SEQ, BLOCKS_DEV * span, HD).astype(jnp.float32)
        device_terms = jnp.einsum('jme,jmh->jeh', group_rows, group_grads).astype(jnp.bfloat16)
        device_terms = lax.optimization_barrier(device_terms)
        grad_sum = grad_sum + lax.optimization_barrier(jnp.sum(device_terms.astype(jnp.float32), axis=0))
        return (grad_sum, (attended.reshape(SEQ_LEN, HD), query_grad.reshape(SEQ_LEN, HD)))
    start_grad = jnp.zeros((ENC_WIDTH, HD), jnp.float32)
    value_weight_grad, outputs = lax.scan(one_sequence, start_grad, (queries, pool, slots, cotangent))
    return (outputs[0], outputs[1], value_weight_grad)
```

```python
import math

import jax
import jax.numpy as jnp
from jax import lax
from jax.experimental import pallas as pl
from jax.experimental.pallas import tpu as pltpu
from jax.sharding import Mesh
from jax.sharding import PartitionSpec as P

HEAD_DIM = 128
BLOCK = 64
SPAN = 256
SCALE = 1.0 / math.sqrt(HEAD_DIM)

AXES = ("yhi", "xh", "xp", "z", "ylo", "core")
SIZES = (4, 2, 2, 8, 2, 2)
SEQ = ("yhi", "xh", "xp")
DP = ("z", "ylo", "core")
N_Z = 8
VMEM = 44 * 1024 * 1024


def route(dx, dy, flip=False):
    pairs = []
    for i in range(math.prod(SIZES)):
        rest, core = divmod(i, 2)
        rest, ylo = divmod(rest, 2)
        rest, z = divmod(rest, N_Z)
        yhi, x = divmod(rest, 4)
        y = (2 * yhi + ylo + dy) % 8
        x = (x + dx) % 4
        core = 1 - core if flip else core
        there = ((((y // 2) * 4 + x) * N_Z + z) * 2 + y % 2) * 2 + core
        pairs.append((i, there))
    return pairs


def send(value, dx, dy, flip=False):
    return lax.ppermute(value, AXES, route(dx, dy, flip))


def after(value, token):
    return lax.optimization_barrier((value, token))[0]


def swap(value):
    return send(value, 0, 0, True)


def next_group(rows):
    n = 16
    return lax.ppermute(rows, SEQ, [(i - 1, i) for i in range(1, n)])


def ordered(first, own, other, axis):
    return jnp.where(
        first, jnp.concatenate([own, other], axis), jnp.concatenate([other, own], axis)
    )


def own_columns(weight, core, xp):
    mine = lax.dynamic_slice(weight, (0, core * 1024 + xp * 512), (28, 512))
    theirs = lax.dynamic_slice(weight, (0, (1 - core) * 1024 + xp * 512), (28, 512))
    return mine, theirs


def gather_z(block):
    copies = jnp.broadcast_to(block[None], (N_Z,) + block.shape)
    return lax.all_to_all(copies, "z", 0, 0)


def spread(part):
    lo, hi = part[:4], part[4:]
    return tuple((send(lo, -dx, -dy), send(hi, dx, dy)) for dx, dy in ((0, 1), (1, 0), (1, 1)))


def whole(part, arrived, ylo, xp):
    by_y, by_x, by_xy = (jnp.concatenate(pair, 0) for pair in arrived)
    same = ordered(xp == 0, part, by_x, 2)
    other = ordered(xp == 0, by_y, by_xy, 2)
    both = ordered(ylo == 0, same[:, None], other[:, None], 1)
    return both.reshape(896, 1024)


def dot(a, b, dims):
    return lax.dot_general(a, b, (dims, ((), ())), preferred_element_type=jnp.float32)


def key_kernel(enc_ref, weight_ref, query_ref, cot_ref, key_ref, prob_ref, term_ref, grad, total):
    step = pl.program_id(0)
    enc = enc_ref[0]
    key_ref[0] = dot(enc, weight_ref[...], ((1,), (0,))).astype(jnp.bfloat16)
    for head in range(8):
        cols = slice(head * HEAD_DIM, (head + 1) * HEAD_DIM)
        scores = dot(query_ref[0, :, cols], key_ref[0, :, cols], ((1,), (1,))) * SCALE
        weights = jnp.exp(scores - jnp.max(scores, axis=-1, keepdims=True))
        probs = weights / jnp.sum(weights, axis=-1, keepdims=True)
        prob_ref[0, head] = probs
        grad[:, cols] = dot(
            probs.astype(jnp.bfloat16), cot_ref[0, :, cols], ((0,), (0,))
        ).astype(jnp.bfloat16)
    term = dot(enc, grad[...], ((0,), (0,)))

    @pl.when(step == 0)
    def _():
        total[...] = term

    @pl.when(step > 0)
    def _():
        total[...] += term

    @pl.when(step == pl.num_programs(0) - 1)
    def _():
        term_ref[...] = total[...].astype(jnp.bfloat16)


def block_spec(*shape):
    return pl.BlockSpec((1,) + shape, lambda i: (i,) + (0,) * len(shape))


def full_spec(*shape):
    return pl.BlockSpec(shape, lambda i: (0,) * len(shape))


def key_part(enc, weight, query, cot):
    return pl.pallas_call(
        key_kernel,
        grid=(4,),
        in_specs=[
            block_spec(SPAN, 896),
            full_spec(896, 1024),
            block_spec(BLOCK, 1024),
            block_spec(BLOCK, 1024),
        ],
        out_specs=[
            block_spec(SPAN, 1024),
            block_spec(8, BLOCK, SPAN),
            full_spec(896, 1024),
        ],
        out_shape=[
            jax.ShapeDtypeStruct((4, SPAN, 1024), jnp.bfloat16),
            jax.ShapeDtypeStruct((4, 8, BLOCK, SPAN), jnp.float32),
            jax.ShapeDtypeStruct((896, 1024), jnp.bfloat16),
        ],
        scratch_shapes=[
            pltpu.VMEM((SPAN, 1024), jnp.bfloat16),
            pltpu.VMEM((896, 1024), jnp.float32),
        ],
        compiler_params=pltpu.CompilerParams(vmem_limit_bytes=VMEM),
        cost_estimate=pl.CostEstimate(
            flops=4_000_000_000, bytes_accessed=12_000_000, transcendentals=524288
        ),
        name="key_part",
    )(enc, weight, query, cot)


def value_kernel(enc_ref, weight_ref, key_ref, prob_ref, cot_ref, att_ref, qgrad_ref, value):
    value[...] = dot(enc_ref[0], weight_ref[...], ((1,), (0,))).astype(jnp.bfloat16)
    for head in range(8):
        cols = slice(head * HEAD_DIM, (head + 1) * HEAD_DIM)
        probs = prob_ref[0, head]
        cot = cot_ref[0, :, cols]
        attended = dot(probs.astype(jnp.bfloat16), value[:, cols], ((1,), (0,)))
        attended = attended.astype(jnp.bfloat16)
        prob_grad = dot(cot, value[:, cols], ((1,), (1,)))
        row_total = jnp.sum(
            cot.astype(jnp.float32) * attended.astype(jnp.float32), axis=-1, keepdims=True
        )
        score_grad = (SCALE * probs * (prob_grad - row_total)).astype(jnp.bfloat16)
        att_ref[0, :, cols] = attended
        qgrad_ref[0, :, cols] = dot(score_grad, key_ref[0, :, cols], ((1,), (0,))).astype(
            jnp.bfloat16
        )


def value_part(enc, weight, keys, probs, cot):
    return pl.pallas_call(
        value_kernel,
        grid=(4,),
        in_specs=[
            block_spec(SPAN, 896),
            full_spec(896, 1024),
            block_spec(SPAN, 1024),
            block_spec(8, BLOCK, SPAN),
            block_spec(BLOCK, 1024),
        ],
        out_specs=[block_spec(BLOCK, 1024), block_spec(BLOCK, 1024)],
        out_shape=[jax.ShapeDtypeStruct((4, BLOCK, 1024), jnp.bfloat16)] * 2,
        scratch_shapes=[pltpu.VMEM((SPAN, 1024), jnp.bfloat16)],
        compiler_params=pltpu.CompilerParams(vmem_limit_bytes=VMEM),
        cost_estimate=pl.CostEstimate(
            flops=2_500_000_000, bytes_accessed=10_000_000, transcendentals=0
        ),
        name="value_part",
    )(enc, weight, keys, probs, cot)


def quarter(term, ylo, xp):
    part = lax.dynamic_slice(term, (0, ylo, 0, xp * 512), (N_Z, 1, 56, 512))
    return part.reshape(N_Z, 56, 512)


def body(queries, pool, slots, key_weight, value_weight, cotangent):
    core, xp, ylo = lax.axis_index("core"), lax.axis_index("xp"), lax.axis_index("ylo")
    bf16, f32 = jnp.bfloat16, jnp.float32

    key_mine, key_theirs = own_columns(key_weight, core, xp)
    value_mine, value_theirs = own_columns(value_weight, core, xp)
    came = swap(jnp.concatenate([key_theirs, value_theirs], 1))
    key_block = ordered(core == 0, key_mine, came[:, :512], 0)
    value_block = ordered(core == 0, value_mine, came[:, 512:], 0)
    key_part_z = gather_z(key_block)
    key_spread = spread(key_part_z)

    rows = jnp.take(pool[0], slots[0].reshape(-1), axis=0).reshape(2, SPAN, 896)
    earlier = jnp.stack([next_group(rows[1]), rows[0]])
    enc = jnp.concatenate([earlier, swap(earlier)])

    def halves(x):
        x = x[0]
        mine = lax.dynamic_slice(x, (0, core * 1024), (128, 1024))
        theirs = lax.dynamic_slice(x, (0, (1 - core) * 1024), (128, 1024))
        return mine, theirs

    query_mine, query_theirs = halves(queries)
    cot_mine, cot_theirs = halves(cotangent)
    token_came = swap(jnp.stack([query_theirs, cot_theirs]))
    query = jnp.concatenate([query_mine, token_came[0]]).reshape(4, BLOCK, 1024)
    cot = jnp.concatenate([cot_mine, token_came[1]]).reshape(4, BLOCK, 1024)

    key_whole = whole(key_part_z, key_spread, ylo, xp)
    keys, probs, term = key_part(enc, key_whole, query, cot)

    term = term.reshape(N_Z, 2, 56, 1024)
    sums = quarter(term, ylo, xp).astype(f32)
    arrived = []
    for dx, dy in ((0, 1), (1, 0), (1, 1)):
        piece = quarter(term, ylo ^ dy, xp ^ dx)
        arrived.append((send(piece[:4], -dx, -dy), send(piece[4:], dx, dy)))

    value_part_z = gather_z(after(value_block, term))
    value_spread = spread(value_part_z)

    for pair in arrived:
        sums = sums + jnp.concatenate(pair, 0).astype(f32)
    along_z = lax.all_to_all(sums.astype(bf16), "z", 0, 0)
    sums = jnp.sum(along_z.astype(f32), axis=0)
    sums = sums.reshape(2, 2, 14, 4, 128).transpose(1, 3, 0, 2, 4)
    left = lax.all_to_all(sums.astype(bf16).reshape(8, 2, 14, 128), ("xh", "yhi"), 0, 0)
    done = jnp.sum(left.astype(f32), axis=0).astype(bf16)
    copies = jnp.broadcast_to(done[None], (16, 2, 14, 128)).reshape(32, 14, 128)
    pieces = lax.all_to_all(copies, ("yhi", "xh", "xp", "core"), 0, 0)
    pieces = pieces.reshape(4, 2, 2, 2, 14, 128).transpose(1, 4, 3, 2, 0, 5)
    weight_grad = pieces.reshape(28, 2048).astype(f32)

    value_whole = whole(value_part_z, value_spread, ylo, xp)
    att, qgrad = value_part(enc, value_whole, keys, probs, cot)
    att, qgrad = att.reshape(2, 128, 1024), qgrad.reshape(2, 128, 1024)
    out_came = swap(jnp.stack([att[1], qgrad[1]]))
    attended = ordered(core == 0, att[0], out_came[0], 1)
    query_grad = ordered(core == 0, qgrad[0], out_came[1], 1)
    return attended[None], query_grad[None], weight_grad


def solution(mesh):
    fine = Mesh(mesh.devices.reshape(SIZES), AXES)
    by_token = P(DP, SEQ, None)
    return jax.shard_map(
        body,
        mesh=fine,
        in_specs=(
            by_token,
            P(DP, SEQ, None, None),
            by_token,
            P(DP, None),
            P(DP, None),
            by_token,
        ),
        out_specs=(by_token, by_token, P(DP, None)),
        check_vma=False,
    )
```

```python
import math

import jax
import jax.numpy as jnp
from jax import lax
from jax.experimental import pallas as pl
from jax.experimental.pallas import tpu as pltpu
from jax.sharding import Mesh
from jax.sharding import PartitionSpec as P

HEAD_DIM = 128
BLOCK = 64
SPAN = 256
SCALE = 1.0 / math.sqrt(HEAD_DIM)

AXES = ("yhi", "xh", "xp", "zh", "zl", "ylo", "core")
SIZES = (4, 2, 2, 4, 2, 2, 2)
SEQ = ("yhi", "xh", "xp")
DP = ("zh", "zl", "ylo", "core")
CUBE = ("zl", "ylo", "xp")
VMEM = 60 * 1024 * 1024


def place(x, y, z, core):
    return (((y // 2 * 4 + x) * 8 + z) * 2 + y % 2) * 2 + core


def odd_square(dx, dy):
    return [
        (
            place(x, y, z, core),
            place((x + dx * (2 * (x % 2) - 1)) % 4, (y + dy * (2 * (y % 2) - 1)) % 8, z, core),
        )
        for x in range(4)
        for y in range(8)
        for z in range(8)
        for core in range(2)
    ]


ODD_SQUARE = [odd_square(1, 0), odd_square(0, 1), odd_square(1, 1)]
ODD_Z = [
    (place(x, y, z, core), place(x, y, (z + 2 * (z % 2) - 1) % 8, core))
    for x in range(4)
    for y in range(8)
    for z in range(8)
    for core in range(2)
]


def after(value, token):
    return lax.optimization_barrier((value, token))[0]


def swap(value):
    return lax.ppermute(value, "core", [(0, 1), (1, 0)])


def next_group(rows):
    n = 16
    return lax.ppermute(rows, SEQ, [(i - 1, i) for i in range(1, n)])


def ordered(first, own, other, axis):
    return jnp.where(
        first, jnp.concatenate([own, other], axis), jnp.concatenate([other, own], axis)
    )


def copies(value, count):
    return jnp.broadcast_to(value[None], (count,) + value.shape)


def dot(a, b, dims):
    return lax.dot_general(a, b, (dims, ((), ())), preferred_element_type=jnp.float32)


def pick(own, other):
    return jnp.where(pl.program_id(0) < 2, own, other)


def key_kernel(
    core_ref, own_ref, other_ref, weight_ref, query_ref, cot_ref, came_ref,
    key_ref, prob_ref, term_ref, total,
):
    step = pl.program_id(0)
    enc = pick(own_ref[0], other_ref[0])
    query = pick(query_ref[0], came_ref[0, 0])
    cot = pick(cot_ref[0], came_ref[1, 0])
    keys = dot(enc, weight_ref[...], ((1,), (0,))).astype(jnp.bfloat16)
    key_ref[0] = keys
    heads = [slice(h * HEAD_DIM, (h + 1) * HEAD_DIM) for h in range(8)]
    scores = [dot(query[:, cols], keys[:, cols], ((1,), (1,))) for cols in heads]
    scores = jnp.concatenate(scores) * SCALE
    weights = jnp.exp(scores - jnp.max(scores, axis=-1, keepdims=True))
    probs = weights * (1.0 / jnp.sum(weights, axis=-1, keepdims=True))
    prob_ref[0] = probs
    low = probs.astype(jnp.bfloat16)
    grads = [
        dot(low[h * BLOCK : (h + 1) * BLOCK], cot[:, cols], ((0,), (0,)))
        for h, cols in enumerate(heads)
    ]
    grads = jnp.concatenate(grads, axis=1).astype(jnp.bfloat16)
    term = dot(enc, grads, ((0,), (0,)))

    @pl.when(step == 0)
    def _():
        total[...] = term

    @pl.when(jnp.logical_and(step > 0, step < 3))
    def _():
        total[...] += term

    @pl.when(step == 3)
    def _():
        total[...] += term
        for zh in range(4):
            for slot in range(8):
                row = (zh * 4 + slot // 2) * 56
                for yhi in range(4):
                    col = slot % 2 * 512 + yhi * 128
                    piece = total[row : row + 56, col : col + 128]
                    term_ref[slot, zh, yhi] = piece.astype(jnp.bfloat16)


def block_spec(*shape):
    return pl.BlockSpec((1,) + shape, lambda i, core: (i,) + (0,) * len(shape))


def full_spec(*shape):
    return pl.BlockSpec(shape, lambda i, core: (0,) * len(shape))


def token_specs():
    own = pl.BlockSpec((1, BLOCK, 1024), lambda i, core: (jnp.minimum(i, 1), 0, core[0]))
    came = pl.BlockSpec((2, 1, BLOCK, 1024), lambda i, core: (0, jnp.maximum(i - 2, 0), 0, 0))
    return own, came


def pair_specs(*shape):
    rest = (0,) * len(shape)
    own = pl.BlockSpec((1,) + shape, lambda i, core: (jnp.minimum(i, 1),) + rest)
    other = pl.BlockSpec((1,) + shape, lambda i, core: (jnp.maximum(i - 2, 0),) + rest)
    return [own, other]


def key_part(core, own, other, weight, queries, cots, came):
    token, came_spec = token_specs()
    return pl.pallas_call(
        key_kernel,
        grid_spec=pltpu.PrefetchScalarGridSpec(
            num_scalar_prefetch=1,
            grid=(4,),
            in_specs=pair_specs(SPAN, 896) + [full_spec(896, 1024), token, token, came_spec],
            out_specs=[
                block_spec(SPAN, 1024),
                block_spec(8 * BLOCK, SPAN),
                full_spec(8, 4, 4, 56, 128),
            ],
            scratch_shapes=[pltpu.VMEM((896, 1024), jnp.float32)],
        ),
        out_shape=[
            jax.ShapeDtypeStruct((4, SPAN, 1024), jnp.bfloat16),
            jax.ShapeDtypeStruct((4, 8 * BLOCK, SPAN), jnp.float32),
            jax.ShapeDtypeStruct((8, 4, 4, 56, 128), jnp.bfloat16),
        ],
        compiler_params=pltpu.CompilerParams(vmem_limit_bytes=VMEM),
        cost_estimate=pl.CostEstimate(
            flops=4_000_000_000, bytes_accessed=12_000_000, transcendentals=524288
        ),
        name="key_part",
    )(core, own, other, weight, queries, cots, came)


def value_kernel(
    core_ref, own_ref, other_ref, weight_ref, key_ref, prob_ref, cot_ref, came_ref,
    mine_ref, theirs_ref,
):
    enc = pick(own_ref[0], other_ref[0])
    cot = pick(cot_ref[0], came_ref[0, 0])
    values = dot(enc, weight_ref[...], ((1,), (0,))).astype(jnp.bfloat16)
    heads = [slice(h * HEAD_DIM, (h + 1) * HEAD_DIM) for h in range(8)]
    rows = [slice(h * BLOCK, (h + 1) * BLOCK) for h in range(8)]
    probs = prob_ref[0]
    low = probs.astype(jnp.bfloat16)
    attended = [dot(low[r], values[:, c], ((1,), (0,))) for r, c in zip(rows, heads)]
    attended = jnp.concatenate(attended, axis=1).astype(jnp.bfloat16)
    prob_grad = [dot(cot[:, c], values[:, c], ((1,), (1,))) for c in heads]
    both = cot.astype(jnp.float32) * attended.astype(jnp.float32)
    row_total = [jnp.sum(both[:, c], axis=-1, keepdims=True) for c in heads]
    score_grad = SCALE * probs * (jnp.concatenate(prob_grad) - jnp.concatenate(row_total))
    score_grad = score_grad.astype(jnp.bfloat16)
    qgrad = [dot(score_grad[r], key_ref[0, :, c], ((1,), (0,))) for r, c in zip(rows, heads)]
    qgrad = jnp.concatenate(qgrad, axis=1).astype(jnp.bfloat16)
    step = pl.program_id(0)

    @pl.when(step < 2)
    def _():
        mine_ref[0, 0] = attended
        mine_ref[0, 1] = qgrad

    @pl.when(step >= 2)
    def _():
        theirs_ref[0, 0] = attended
        theirs_ref[0, 1] = qgrad


def value_part(core, own, other, weight, keys, probs, cots, came):
    token, _ = token_specs()
    came_spec = pl.BlockSpec((1, 1, BLOCK, 1024), lambda i, core: (1, jnp.maximum(i - 2, 0), 0, 0))
    return pl.pallas_call(
        value_kernel,
        grid_spec=pltpu.PrefetchScalarGridSpec(
            num_scalar_prefetch=1,
            grid=(4,),
            in_specs=pair_specs(SPAN, 896)
            + [
                full_spec(896, 1024),
                block_spec(SPAN, 1024),
                block_spec(8 * BLOCK, SPAN),
                token,
                came_spec,
            ],
            out_specs=pair_specs(2, BLOCK, 1024),
        ),
        out_shape=[jax.ShapeDtypeStruct((2, 2, BLOCK, 1024), jnp.bfloat16)] * 2,
        compiler_params=pltpu.CompilerParams(vmem_limit_bytes=VMEM),
        cost_estimate=pl.CostEstimate(
            flops=2_500_000_000, bytes_accessed=10_000_000, transcendentals=0
        ),
        name="value_part",
    )(core, own, other, weight, keys, probs, cots, came)


def body(queries, pool, slots, key_weight, value_weight, cotangent):
    core, xp = lax.axis_index("core"), lax.axis_index("xp")
    ylo, zl = lax.axis_index("ylo"), lax.axis_index("zl")
    which = core.astype(jnp.int32).reshape(1)
    bf16, f32 = jnp.bfloat16, jnp.float32

    def columns(weight, core):
        return lax.dynamic_slice(weight, (0, core * 1024 + xp * 512), (28, 512))

    weights = (key_weight, value_weight)
    mine = jnp.concatenate([columns(w, core) for w in weights], 1)
    came = swap(jnp.concatenate([columns(w, 1 - core) for w in weights], 1))
    block = copies(ordered(core == 0, mine, came, 0), 4)

    along = lax.all_to_all(block, "zh", 0, 0)
    key_z, value_z = along[:, :, :512], along[:, :, 512:]

    slots, queries, cotangent = after((slots, queries, cotangent), block)
    rows = jnp.take(pool[0], slots[0].reshape(-1), axis=0).reshape(2, SPAN, 896)
    own = jnp.stack([next_group(rows[1]), rows[0]])
    other = swap(own)
    theirs = [lax.dynamic_slice(v[0], (0, (1 - core) * 1024), (128, 1024)) for v in (queries, cotangent)]
    tokens = swap(jnp.stack(theirs)).reshape(2, 2, BLOCK, 1024)
    queries, cotangent = queries.reshape(2, BLOCK, 2048), cotangent.reshape(2, BLOCK, 2048)

    key_copies = copies(after(key_z, own), 8)
    cube = lax.all_to_all(key_copies, CUBE, 0, 0).reshape(2, 2, 2, 4, 56, 512)
    cube = jnp.concatenate([cube[:, :, 0], cube[:, :, 1]], axis=-1)
    key_whole = cube.transpose(2, 0, 1, 3, 4).reshape(896, 1024)
    value_z = after(value_z, key_copies)
    value_z = ordered(zl == 0, value_z[:, None], lax.ppermute(value_z, AXES, ODD_Z)[:, None], 1)
    value_z = value_z.reshape(8, 56, 512)
    key_whole, value_z = lax.optimization_barrier((key_whole, value_z))
    keys, probs, term = key_part(which, own, other, key_whole, queries, cotangent, tokens)

    cube = lax.all_to_all(term, CUBE, 0, 0)
    value_z = after(value_z, term)
    around = [lax.ppermute(value_z, AXES, pairs) for pairs in ODD_SQUARE]
    sums = jnp.sum(cube.astype(f32), axis=0).astype(bf16).reshape(16, 56, 128)
    by_x, by_y, by_xy = after(around, sums)
    along = lax.all_to_all(sums, ("zh", "yhi"), 0, 0)
    same = ordered(xp == 0, value_z, by_x, 2)
    across = ordered(xp == 0, by_y, by_xy, 2)
    value_whole = ordered(ylo == 0, same[:, None], across[:, None], 1).reshape(896, 1024)
    mine, theirs = value_part(which, own, other, value_whole, keys, probs, cotangent, tokens)

    done = jnp.sum(along.astype(f32), axis=0).astype(bf16).reshape(2, 1, 28, 128)
    done = jnp.broadcast_to(done, (2, 16, 28, 128)).reshape(32, 28, 128)
    pieces = lax.all_to_all(done, ("core", "xh", "xp", "yhi"), 0, 0)
    pieces = pieces.reshape(2, 2, 2, 4, 28, 128).astype(f32)
    weight_grad = jnp.sum(pieces, axis=1).transpose(3, 0, 1, 2, 4).reshape(28, 2048)

    came = swap(after(theirs, done))
    attended = ordered(core == 0, mine[:, 0], came[:, 0], 2)
    query_grad = ordered(core == 0, mine[:, 1], came[:, 1], 2)
    return attended.reshape(1, 128, 2048), query_grad.reshape(1, 128, 2048), weight_grad


def solution(mesh):
    fine = Mesh(mesh.devices.reshape(SIZES), AXES)
    by_token = P(DP, SEQ, None)
    return jax.shard_map(
        body,
        mesh=fine,
        in_specs=(
            by_token,
            P(DP, SEQ, None, None),
            by_token,
            P(DP, None),
            P(DP, None),
            by_token,
        ),
        out_specs=(by_token, by_token, P(DP, None)),
        check_vma=False,
    )
```

```python
import math

import jax
import jax.numpy as jnp
from jax import lax
from jax.experimental import pallas as pl
from jax.experimental.pallas import tpu as pltpu
from jax.sharding import Mesh
from jax.sharding import PartitionSpec as P

HEAD_DIM = 128
BLOCK = 64
SPAN = 256
SCALE = 1.0 / math.sqrt(HEAD_DIM)

AXES = ("yhi", "xh", "xp", "zh", "zl", "ylo", "core")
SIZES = (4, 2, 2, 4, 2, 2, 2)
SEQ = ("yhi", "xh", "xp")
DP = ("zh", "zl", "ylo", "core")
CUBE = ("zl", "ylo", "xp")
VMEM = 60 * 1024 * 1024


def place(x, y, z, core):
    return (((y // 2 * 4 + x) * 8 + z) * 2 + y % 2) * 2 + core


def odd_square(dx, dy):
    return [
        (
            place(x, y, z, core),
            place((x + dx * (2 * (x % 2) - 1)) % 4, (y + dy * (2 * (y % 2) - 1)) % 8, z, core),
        )
        for x in range(4)
        for y in range(8)
        for z in range(8)
        for core in range(2)
    ]


ODD_SQUARE = [odd_square(1, 0), odd_square(0, 1), odd_square(1, 1)]
ODD_Z = [
    (place(x, y, z, core), place(x, y, (z + 2 * (z % 2) - 1) % 8, core))
    for x in range(4)
    for y in range(8)
    for z in range(8)
    for core in range(2)
]


def after(value, token):
    return lax.optimization_barrier((value, token))[0]


def swap(value):
    return lax.ppermute(value, "core", [(0, 1), (1, 0)])


def next_group(rows):
    n = 16
    return lax.ppermute(rows, SEQ, [(i - 1, i) for i in range(1, n)])


def ordered(first, own, other, axis):
    return jnp.where(
        first, jnp.concatenate([own, other], axis), jnp.concatenate([other, own], axis)
    )


def copies(value, count):
    return jnp.broadcast_to(value[None], (count,) + value.shape)


def dot(a, b, dims):
    return lax.dot_general(a, b, (dims, ((), ())), preferred_element_type=jnp.float32)


def in_rows(pieces):
    return jnp.concatenate([p.astype(jnp.float32) for p in pieces]).astype(jnp.bfloat16)


def project(own_ref, other_ref, weight):
    both = [dot(ref[...], weight, ((1,), (0,))) for ref in (own_ref, other_ref)]
    return jnp.concatenate([x.astype(jnp.bfloat16) for x in both])


PAIRS = [(block, slice(h * HEAD_DIM, (h + 1) * HEAD_DIM)) for block in range(4) for h in range(2)]


def rows_of(block):
    return slice(block * SPAN, (block + 1) * SPAN)


def token_rows(own_ref, came_ref, kind):
    tiles = [own_ref[0], own_ref[1], came_ref[kind, 0], came_ref[kind, 1]]
    return [tiles[block][:, cols] for block, cols in PAIRS]


def side_by_side(tiles):
    return jnp.concatenate([jnp.concatenate(tiles[i : i + 2], axis=1) for i in range(0, 8, 2)])


def key_kernel(
    where_ref, own_ref, other_ref, weight_ref, query_ref, cot_ref, came_ref,
    key_ref, prob_ref, term_ref, turned,
):
    @pl.when(pl.program_id(0) == 0)
    def _():
        turned[:, :512] = own_ref[...].T
        turned[:, 512:] = other_ref[...].T

    weight = in_rows(
        [weight_ref[zl, ylo, 0, zh] for zh in range(4) for zl in range(2) for ylo in range(2)]
    )
    keys = project(own_ref, other_ref, weight)
    key_ref[...] = keys
    query = token_rows(query_ref, came_ref, 0)
    cot = token_rows(cot_ref, came_ref, 1)
    scores = [
        dot(q, keys[rows_of(block), cols], ((1,), (1,))) for q, (block, cols) in zip(query, PAIRS)
    ]
    scores = jnp.concatenate(scores) * SCALE
    weights = jnp.exp(scores - jnp.max(scores, axis=-1, keepdims=True))
    probs = weights * (1.0 / jnp.sum(weights, axis=-1, keepdims=True))
    low = probs.astype(jnp.bfloat16)
    prob_ref[0] = low
    grads = [dot(low[i * BLOCK : (i + 1) * BLOCK], cot[i], ((0,), (0,))) for i in range(8)]
    grads = side_by_side([x.astype(jnp.bfloat16) for x in grads])
    term = dot(turned[...], grads, ((1,), (0,))).astype(jnp.float32)
    for zh in range(4):
        for slot in range(4):
            row = (zh * 4 + slot) * 56
            for half in range(2):
                piece = term[row : row + 56, half * 128 : (half + 1) * 128]
                term_ref[slot, 0, zh, 0, half] = piece.astype(jnp.bfloat16)


def value_kernel(
    where_ref, own_ref, other_ref, here_ref, across_ref, key_ref, prob_ref,
    cot_ref, came_ref, att_ref, qgrad_ref, theirs_ref,
):
    odd = where_ref[1] == 1
    here, across = here_ref[...], across_ref[...]
    first, second = jnp.where(odd, across, here), jnp.where(odd, here, across)
    weight = in_rows([half[z] for z in range(8) for half in (first, second)])
    values = project(own_ref, other_ref, weight)
    low = prob_ref[0]
    cot = token_rows(cot_ref, came_ref, 0)
    low_tiles = [low[i * BLOCK : (i + 1) * BLOCK] for i in range(8)]
    value_tiles = [values[rows_of(block), cols] for block, cols in PAIRS]
    attended = [
        dot(p, v, ((1,), (0,))).astype(jnp.bfloat16) for p, v in zip(low_tiles, value_tiles)
    ]
    prob_grad = [dot(g, v, ((1,), (1,))) for g, v in zip(cot, value_tiles)]
    both = jnp.concatenate(cot).astype(jnp.float32) * jnp.concatenate(attended).astype(jnp.float32)
    row_total = jnp.sum(both, axis=-1, keepdims=True)
    score_grad = SCALE * low.astype(jnp.float32) * (jnp.concatenate(prob_grad) - row_total)
    score_grad = score_grad.astype(jnp.bfloat16)
    query_grad = [
        dot(score_grad[i * BLOCK : (i + 1) * BLOCK], key_ref[rows_of(block), cols], ((1,), (0,)))
        for i, (block, cols) in enumerate(PAIRS)
    ]
    for i, (block, cols) in enumerate(PAIRS):
        qgrad = query_grad[i].astype(jnp.bfloat16)
        if block < 2:
            att_ref[block, :, cols] = attended[i]
            qgrad_ref[block, :, cols] = qgrad
        else:
            theirs_ref[0, block - 2, :, cols] = attended[i]
            theirs_ref[1, block - 2, :, cols] = qgrad


def full_spec(*shape):
    return pl.BlockSpec(shape, lambda j, where: (0,) * len(shape))


def columns_spec(*shape):
    return pl.BlockSpec(shape, lambda j, where: (0,) * (len(shape) - 1) + (j,))


def half_spec(*shape):
    return pl.BlockSpec(shape, lambda j, where: (0,) * (len(shape) - 1) + (j % 2,))


def own_tokens():
    return pl.BlockSpec((2, BLOCK, 256), lambda j, where: (0, 0, where[0] * 4 + j))


def prob_spec():
    return pl.BlockSpec((1, 512, SPAN), lambda j, where: (j, 0, 0))


PARAMS = pltpu.CompilerParams(vmem_limit_bytes=VMEM)


def key_part(where, own, other, weight, queries, cots, came):
    return pl.pallas_call(
        key_kernel,
        grid_spec=pltpu.PrefetchScalarGridSpec(
            num_scalar_prefetch=1,
            grid=(4,),
            in_specs=[
                full_spec(512, 896),
                full_spec(512, 896),
                pl.BlockSpec(
                    (2, 2, 1, 4, 56, 256), lambda j, where: (0, 0, j // 2, 0, 0, j % 2)
                ),
                own_tokens(),
                own_tokens(),
                columns_spec(2, 2, BLOCK, 256),
            ],
            out_specs=[
                columns_spec(1024, 256),
                prob_spec(),
                pl.BlockSpec(
                    (4, 1, 4, 1, 2, 56, 128), lambda j, where: (0, j // 2, 0, j % 2, 0, 0, 0)
                ),
            ],
            scratch_shapes=[pltpu.VMEM((896, 1024), jnp.bfloat16)],
        ),
        out_shape=[
            jax.ShapeDtypeStruct((1024, 1024), jnp.bfloat16),
            jax.ShapeDtypeStruct((4, 512, SPAN), jnp.bfloat16),
            jax.ShapeDtypeStruct((4, 2, 4, 2, 2, 56, 128), jnp.bfloat16),
        ],
        compiler_params=PARAMS,
        cost_estimate=pl.CostEstimate(
            flops=4_000_000_000, bytes_accessed=10_000_000, transcendentals=524288
        ),
        name="key_part",
    )(where, own, other, weight, queries, cots, came)


def value_part(far, where, own, other, weights, keys, probs, cots, came):
    def at(i, where):
        return 2 * (where[2] ^ far) + i

    return pl.pallas_call(
        value_kernel,
        grid_spec=pltpu.PrefetchScalarGridSpec(
            num_scalar_prefetch=1,
            grid=(2,),
            in_specs=[full_spec(512, 896), full_spec(512, 896)]
            + [columns_spec(8, 56, 256)] * 2
            + [
                pl.BlockSpec((1024, 256), lambda i, where: (0, at(i, where))),
                pl.BlockSpec((1, 512, SPAN), lambda i, where: (at(i, where), 0, 0)),
                pl.BlockSpec((2, BLOCK, 256), lambda i, where: (0, 0, where[0] * 4 + at(i, where))),
                pl.BlockSpec((1, 2, BLOCK, 256), lambda i, where: (1, 0, 0, at(i, where))),
            ],
            out_specs=[columns_spec(2, BLOCK, 256)] * 2 + [columns_spec(2, 2, BLOCK, 256)],
        ),
        out_shape=[
            jax.ShapeDtypeStruct((2, BLOCK, 512), jnp.bfloat16),
            jax.ShapeDtypeStruct((2, BLOCK, 512), jnp.bfloat16),
            jax.ShapeDtypeStruct((2, 2, BLOCK, 512), jnp.bfloat16),
        ],
        compiler_params=PARAMS,
        cost_estimate=pl.CostEstimate(
            flops=1_250_000_000, bytes_accessed=6_000_000, transcendentals=0
        ),
        name="value_part",
    )(where, own, other, *weights, keys, probs, cots, came)


def copy_kernel(slots_ref, pool_ref, rows_ref):
    rows_ref[...] = pool_ref[0, 0]


def chosen(slots, pool, block):
    return pl.pallas_call(
        copy_kernel,
        grid_spec=pltpu.PrefetchScalarGridSpec(
            num_scalar_prefetch=1,
            grid=(2,),
            in_specs=[
                pl.BlockSpec((1, 1, 128, 896), lambda i, slots: (0, slots[0, block, i], 0, 0))
            ],
            out_specs=pl.BlockSpec((128, 896), lambda i, slots: (i, 0)),
        ),
        out_shape=jax.ShapeDtypeStruct((SPAN, 896), jnp.bfloat16),
        compiler_params=PARAMS,
        cost_estimate=pl.CostEstimate(flops=0, bytes_accessed=900_000, transcendentals=0),
        name="chosen",
    )(slots, pool)


def body(queries, pool, slots, key_weight, value_weight, cotangent):
    core, xp = lax.axis_index("core"), lax.axis_index("xp")
    ylo, zl = lax.axis_index("ylo"), lax.axis_index("zl")
    where = jnp.stack([core, ylo, xp]).astype(jnp.int32)
    bf16, f32 = jnp.bfloat16, jnp.float32

    def columns(weight, core):
        return lax.dynamic_slice(weight, (0, core * 1024 + xp * 512), (28, 512))

    last = chosen(slots, pool, 1)
    arrived = next_group(last)
    weights = after((key_weight, value_weight), last)
    mine = jnp.concatenate([columns(w, core) for w in weights], 1)
    came = swap(jnp.concatenate([columns(w, 1 - core) for w in weights], 1))
    block = copies(ordered(core == 0, mine, came, 0), 4)

    along = lax.all_to_all(block, "zh", 0, 0)
    key_z, value_z = along[:, :, :512], along[:, :, 512:]

    slots = after(slots, (block, arrived))
    first = chosen(slots, pool, 0)
    own = jnp.concatenate([arrived, first])
    queries, cotangent = after((queries, cotangent), arrived)
    theirs = [lax.dynamic_slice(v[0], (0, (1 - core) * 1024), (128, 1024)) for v in (queries, cotangent)]
    tokens = swap(jnp.stack(theirs)).reshape(2, 2, BLOCK, 1024)
    queries, cotangent = queries.reshape(2, BLOCK, 2048), cotangent.reshape(2, BLOCK, 2048)

    key_copies = copies(after(key_z, (first, tokens)), 8)
    cube = lax.all_to_all(key_copies, CUBE, 0, 0).reshape(2, 2, 2, 4, 56, 512)
    value_z = after(value_z, key_copies)
    value_z = ordered(zl == 0, value_z[:, None], lax.ppermute(value_z, AXES, ODD_Z)[:, None], 1)
    value_z = value_z.reshape(8, 56, 512)
    other = swap(after(own, value_z))
    around = [lax.ppermute(value_z, AXES, pairs) for pairs in ODD_SQUARE[:2]]
    cube, value_z = lax.optimization_barrier((cube, value_z))
    keys, probs, term = key_part(where, own, other, cube, queries, cotangent, tokens)

    term, around = lax.optimization_barrier((term, around))
    cube = lax.all_to_all(term.reshape(8, 16, 56, 128), CUBE, 0, 0)
    around.append(lax.ppermute(after(value_z, term), AXES, ODD_SQUARE[2]))
    by_x, by_y, by_xy = around
    rest = (keys, probs, cotangent, tokens)
    near = value_part(0, where, own, other, (value_z, by_y), *rest)
    near_came = swap(near[2])
    sums = jnp.sum(cube.astype(f32), axis=0).astype(bf16)
    sums, near, near_came = lax.optimization_barrier((sums, near, near_came))
    along = lax.all_to_all(sums, ("zh", "yhi"), 0, 0)
    by_x, by_xy = after((by_x, by_xy), sums)
    far = value_part(1, where, own, other, (by_x, by_xy), *rest)
    along = after(along, far)
    done = jnp.sum(along.astype(f32), axis=0).astype(bf16).reshape(2, 1, 28, 128)
    done = jnp.broadcast_to(done, (2, 16, 28, 128)).reshape(32, 28, 128)
    pieces = lax.all_to_all(done, ("core", "xh", "xp", "yhi"), 0, 0)
    far_came = swap(far[2])
    near, far, near_came, far_came = after((near, far, near_came, far_came), done)

    def outputs(kind):
        mine = ordered(xp == 0, near[kind], far[kind], 2)
        came = ordered(xp == 0, near_came[kind], far_came[kind], 2)
        return ordered(core == 0, mine, came, 2).reshape(1, 128, 2048)

    pieces = pieces.reshape(2, 2, 2, 4, 28, 128).astype(f32)
    weight_grad = jnp.sum(pieces, axis=1).transpose(3, 0, 1, 2, 4).reshape(28, 2048)
    return outputs(0), outputs(1), weight_grad


def solution(mesh):
    fine = Mesh(mesh.devices.reshape(SIZES), AXES)
    by_token = P(DP, SEQ, None)
    return jax.shard_map(
        body,
        mesh=fine,
        in_specs=(
            by_token,
            P(DP, SEQ, None, None),
            by_token,
            P(DP, None),
            P(DP, None),
            by_token,
        ),
        out_specs=(by_token, by_token, P(DP, None)),
        check_vma=False,
    )
```
